512 devices in a mesh: dp: 64 (over z_hi, x, y, core), head: 8 (over z_lo).
Axes of the slice: x: 4, y: 4, z: 16 (z_hi: 2, z_lo: 8; z = z_hi * 8 + z_lo), core: 2. Of those that a mesh axis runs over, the one named last changes fastest.
Arguments:
- queries: bfloat16 [65536, 8192], P('dp', 'head'), may hold values from -48 to 48
- keys: bfloat16 [65536, 1024], P('dp', 'head'), may hold values from -4 to 4
- values: bfloat16 [65536, 1024], P('dp', 'head'), may hold values from -6 to 6
- segments: int32 [64, 1024], P('dp'), may hold values from 0 to 1023, as said below
Outputs:
- attended: bfloat16 [65536, 8192], P(('dp', 'head'))
The draws below stay inside these ranges and needn't reach their ends.
Inputs may be any that keep to these rules, and one draw needn't show every extreme that they name: `segments`: in every row the ids start at 0 and never fall; a document is a run of equal ids. A replica whose index has an even number of one bits starts all its documents within its first 256 tokens; any other replica starts a document at every multiple of 256. Some replica consists of 1024 documents of one token each.
All inputs are finite; a program needn't handle non-finite values.
Results may differ from the reference program's by a relative error of at most 0.0021.
Values may be sent and summed in bfloat16 or wider, within the bound.
A program may use at most 128 MiB of HBM per device.

```python
import jax
import jax.numpy as jnp
from jax import lax

HD = 128
GROUP = 8
BLK = 256
KVH = 8
TOK = 1024
REPLICAS = 64
TOKENS = 65536


def shared_vectors(key):
    base = jax.random.fold_in(key, 11)
    first, second = jax.random.split(base, 2)
    key_part = jnp.clip(jax.random.normal(first, (TOKENS, KVH, HD), jnp.float32), -4.0, 4.0)
    query_part = jnp.clip(jax.random.normal(second, (TOKENS, KVH, GROUP, HD), jnp.float32), -4.0, 4.0)
    return (query_part.reshape(TOKENS, KVH * GROUP * HD), key_part.reshape(TOKENS, KVH * HD))


def draw_queries(key, part):
    return shared_vectors(key)[0].astype(jnp.bfloat16)


def draw_keys(key, part):
    return shared_vectors(key)[1].astype(jnp.bfloat16)


def bit_parity(numbers):
    total = jnp.zeros_like(numbers)
    for bit_number in range(16):
        total = total + jnp.bitwise_and(jnp.right_shift(numbers, bit_number), 1)
    return jnp.bitwise_and(total, 1)


def draw_segments(key, part):
    base = jax.random.fold_in(key, 5)
    first, second, third = jax.random.split(base, 3)
    replica_ids = jnp.arange(REPLICAS, dtype=jnp.int32)[:, None]
    heavy = bit_parity(replica_ids) == 0
    single_row = jax.random.randint(third, (), 0, REPLICAS).astype(jnp.int32)
    single_row = jnp.bitwise_xor(single_row, 1 - bit_parity(single_row))
    exponent = jax.random.randint(first, (REPLICAS, 1), 1, 4)
    raw_bits = jax.random.randint(second, (REPLICAS, TOK), 0, 1 << 20)
    positions = jnp.arange(TOK, dtype=jnp.int32)[None, :]
    masking = jnp.left_shift(jnp.ones_like(exponent), exponent) - 1
    light_start = (jnp.bitwise_and(raw_bits, masking) == 0) | (positions % BLK == 0)
    heavy_start = (jnp.bitwise_and(raw_bits, 3) == 0) & (positions < BLK)
    starting = jnp.where(heavy, heavy_start, light_start)
    starting = jnp.where(replica_ids == single_row, True, starting)
    starting = jnp.where(positions == 0, False, starting)
    return jnp.cumsum(starting.astype(jnp.int32), axis=1).astype(jnp.int32)


def steps_of(own_key, extent, shards, smallest, largest):
    factor_of, own = 1.0, jax.random.fold_in(own_key, 6)
    for axis_at, blocks in shards:
        heights = jnp.exp(jax.random.uniform(jax.random.fold_in(own, axis_at), (blocks,), jnp.float32, smallest / len(shards), largest / len(shards)))
        factor_of = factor_of * jnp.repeat(heights, extent[axis_at] // blocks).reshape([-1 if axis == axis_at else 1 for axis in range(len(extent))])
    return factor_of


def centred(stream_key, dims, width, limit, pieces=(), kind=jnp.bfloat16):
    gain = steps_of(stream_key, dims, pieces, -0.22, 0.18) if pieces else 1.0
    drawn = jax.random.normal(stream_key, dims, jnp.float32) * width * gain
    return jnp.minimum(jnp.maximum(drawn, -limit), limit).astype(kind)


def setup_inputs(seed: int = 0) -> dict:
    streams_of = jax.random.split(jax.random.key(seed), 5)
    queries = draw_queries(jax.random.fold_in(streams_of[4], 71), 0)
    keys = draw_keys(jax.random.fold_in(streams_of[4], 71), 0)
    values = centred(streams_of[2], (TOKENS, KVH * HD), 1.0, 6.0, ((0, 64), (1, 8)))
    segments = draw_segments(jax.random.fold_in(streams_of[4], 71), 0)
    return {"queries": queries, "keys": keys, "values": values, "segments": segments}


def reference(queries, keys, values, segments):
    scale_factor = HD ** -0.5

    def one_replica(packed):
        query_rows, key_rows, value_rows, segment_row = packed
        query_heads = query_rows.reshape(TOK, KVH, GROUP, HD).astype(jnp.float32).transpose(1, 0, 2, 3)
        key_heads = key_rows.reshape(TOK, KVH, HD).astype(jnp.float32).transpose(1, 0, 2)
        value_heads = value_rows.reshape(TOK, KVH, HD).astype(jnp.float32).transpose(1, 0, 2)
        positions = jnp.arange(TOK, dtype=jnp.int32)
        allowed = (segment_row[None, :] == segment_row[:, None]) & (positions[None, :] <= positions[:, None])

        def one_head(head_pack):
            query_head, key_head, value_head = head_pack
            scores = jnp.einsum("qgd,kd->qgk", query_head, key_head) * scale_factor
            scores = jnp.where(allowed[:, None, :], scores, -1e30)
            row_max = jnp.max(scores, axis=-1, keepdims=True)
            weights = jnp.exp(scores - row_max)
            denominator = jnp.sum(weights, axis=-1)
            rounded = lax.optimization_barrier(weights.astype(jnp.bfloat16)).astype(jnp.float32)
            combined = jnp.einsum("qgk,kd->qgd", rounded, value_head)
            return (combined / denominator[..., None]).astype(jnp.bfloat16)

        per_head = lax.map(one_head, (query_heads, key_heads, value_heads))
        return per_head.transpose(1, 0, 2, 3).reshape(TOK, KVH * GROUP * HD)

    result = lax.map(one_replica, (queries.reshape(REPLICAS, TOK, KVH * GROUP * HD), keys.reshape(REPLICAS, TOK, KVH * HD), values.reshape(REPLICAS, TOK, KVH * HD), segments))
    return result.reshape(TOKENS, KVH * GROUP * HD)
```

```python
import jax
import jax.numpy as jnp
from jax import lax
from jax.experimental import pallas as pl
from jax.experimental.pallas import tpu as pltpu
from jax.sharding import PartitionSpec as P

HEADS = 8
WIDTH = 128
GROUP = 8
BLK = 256
PIECE = 32
MESH = pl.DeviceIdType.MESH
LOG2E = 1.4426950408889634


def xor(a, b):
    total = 0
    for bit in (1, 2, 4):
        total = total + bit * (((a // bit) % 2 + (b // bit) % 2) % 2)
    return total


def step_offset(step):
    even = 1 - step % 2
    return even * (4 + step // 2) + (1 - even) * (((step + 1) // 2) % 4)


def kernel(
    q_hbm, k_hbm, v_hbm, seg_ref, out_ref,
    q_ref, k_ref, v_ref, seg_col, sent, q_sem, kv_sem, send_sem, recv_sem,
):
    tokens, width = q_ref.shape
    chunk = tokens // HEADS
    pieces = chunk // PIECE
    scale = WIDTH**-0.5 * LOG2E
    me = lax.axis_index("head")
    replica = lax.axis_index("dp")
    ones = 0
    for bit in range(16):
        ones = ones + (replica // 2**bit) % 2
    light = ones % 2

    def q_copy(step):
        rows = pl.ds(pl.multiple_of(xor(me, step_offset(step)) * chunk, chunk), chunk)
        return pltpu.make_async_copy(q_hbm.at[rows], q_ref.at[rows], q_sem.at[step])

    k_copy = pltpu.make_async_copy(k_hbm, k_ref, kv_sem.at[0])
    v_copy = pltpu.make_async_copy(v_hbm, v_ref, kv_sem.at[1])
    barrier = pltpu.get_barrier_semaphore()
    for offset in range(1, HEADS):
        pl.semaphore_signal(
            barrier, inc=1, device_id={"head": xor(me, offset)}, device_id_type=MESH
        )
    q_copy(0).start()
    k_copy.start()
    v_copy.start()
    for step in range(1, HEADS):
        q_copy(step).start()
    for part in range(tokens // 128):
        row = seg_ref[0:1, part * 128 : (part + 1) * 128]
        seg_col[part * 128 : (part + 1) * 128, :] = jnp.broadcast_to(row, (128, 128)).T
    k_copy.wait()
    v_copy.wait()
    pl.semaphore_wait(barrier, HEADS - 1)

    def piece_copy(step, piece):
        offset = step_offset(step)
        partner = xor(me, offset)
        source = pl.ds(pl.multiple_of(partner * chunk + piece * PIECE, PIECE), PIECE)
        return pltpu.make_async_remote_copy(
            src_ref=sent.at[source],
            dst_ref=out_ref.at[
                pl.ds(pl.multiple_of(piece * PIECE, PIECE), PIECE),
                pl.ds(pl.multiple_of(me * width, width), width),
            ],
            send_sem=send_sem.at[step, piece],
            recv_sem=recv_sem.at[step, piece],
            device_id={"head": partner},
            device_id_type=MESH,
        )

    def attend(first, key_first, blocks):
        keys = blocks * BLK
        rows = pl.ds(first, PIECE)
        window = pl.ds(key_first, keys)
        queries = jnp.concatenate(
            [q_ref[rows, g * WIDTH : (g + 1) * WIDTH] for g in range(GROUP)], axis=0
        )
        scores = lax.dot_general(
            queries, k_ref[window, :], (((1,), (1,)), ((), ())),
            preferred_element_type=jnp.float32,
        )
        own = seg_col[rows, :]
        own = jnp.concatenate([own] * (keys // 128), axis=1)
        key_seg = seg_ref[0:1, window]
        key_at = key_first + lax.broadcasted_iota(jnp.int32, (PIECE, keys), 1)
        own_at = first + lax.broadcasted_iota(jnp.int32, (PIECE, keys), 0)
        allowed = (own == key_seg) & (key_at <= own_at)
        bias = jnp.where(allowed, 0.0, -jnp.inf)
        scores = scores.reshape(GROUP, PIECE, keys) + bias[None]
        row_max = jnp.max(scores, axis=-1, keepdims=True)
        weights = jnp.exp2((scores - row_max) * scale)
        total = jnp.sum(weights, axis=-1, keepdims=True)
        mixed = jnp.dot(
            weights.astype(jnp.bfloat16).reshape(GROUP * PIECE, keys), v_ref[window, :],
            preferred_element_type=jnp.float32,
        )
        mixed = mixed.reshape(GROUP, PIECE, WIDTH) / total
        for g in range(GROUP):
            sent[rows, g * WIDTH : (g + 1) * WIDTH] = mixed[g].astype(jnp.bfloat16)

    def one_step(step, carry):
        partner = xor(me, step_offset(step))
        q_copy(step).wait()
        block = partner // (BLK // chunk)
        blocks = light + (1 - light) * (block + 1)
        key_first = pl.multiple_of(light * block * BLK, BLK)

        def one_piece(piece, inner):
            first = pl.multiple_of(partner * chunk + piece * PIECE, PIECE)
            for count in range(1, tokens // BLK + 1):

                @pl.when(blocks == count)
                def _(count=count):
                    attend(first, key_first if count == 1 else 0, count)

            @pl.when(step < HEADS - 1)
            def _():
                piece_copy(step, piece).start()

            return inner

        return lax.fori_loop(0, pieces, one_piece, carry)

    lax.fori_loop(0, HEADS, one_step, 0)
    mine = pl.ds(pl.multiple_of(me * chunk, chunk), chunk)
    home = pltpu.make_async_copy(
        sent.at[mine],
        out_ref.at[:, pl.ds(pl.multiple_of(me * width, width), width)],
        kv_sem.at[0],
    )
    home.start()
    home.wait()

    def finish(step, carry):
        def one_piece(piece, inner):
            copy = piece_copy(step, piece)
            copy.wait_send()
            copy.wait_recv()
            return inner

        return lax.fori_loop(0, pieces, one_piece, carry)

    lax.fori_loop(0, HEADS - 1, finish, 0)


def on_device(queries, keys, values, segments):
    tokens, width = queries.shape
    chunk = tokens // HEADS
    pieces = chunk // PIECE
    return pl.pallas_call(
        kernel,
        out_shape=jax.ShapeDtypeStruct((chunk, HEADS * width), queries.dtype),
        in_specs=[pl.BlockSpec(memory_space=pl.ANY)] * 3
        + [pl.BlockSpec(memory_space=pltpu.VMEM)],
        out_specs=pl.BlockSpec(memory_space=pl.ANY),
        scratch_shapes=[
            pltpu.VMEM(queries.shape, queries.dtype),
            pltpu.VMEM(keys.shape, keys.dtype),
            pltpu.VMEM(values.shape, values.dtype),
            pltpu.VMEM((tokens, 128), jnp.int32),
            pltpu.VMEM(queries.shape, queries.dtype),
            pltpu.SemaphoreType.DMA((HEADS,)),
            pltpu.SemaphoreType.DMA((2,)),
            pltpu.SemaphoreType.DMA((HEADS - 1, pieces)),
            pltpu.SemaphoreType.DMA((HEADS - 1, pieces)),
        ],
        compiler_params=pltpu.CompilerParams(
            collective_id=0, has_side_effects=True, vmem_limit_bytes=40 * 2**20
        ),
        cost_estimate=pl.CostEstimate(
            flops=4 * tokens * width * tokens, bytes_accessed=5 * 2**20,
            transcendentals=tokens * GROUP * tokens,
        ),
    )(queries, keys, values, segments)


def solution(mesh):
    placed = (P("dp", "head"), P("dp", "head"), P("dp", "head"), P("dp", None))
    return jax.shard_map(
        on_device, mesh=mesh, in_specs=placed, out_specs=P(("dp", "head"), None), check_vma=False
    )
```

```python
import jax
import jax.numpy as jnp
from jax import lax
from jax.experimental import pallas as pl
from jax.experimental.pallas import tpu as pltpu
from jax.sharding import PartitionSpec as P

HEADS = 8
WIDTH = 128
GROUP = 8
BLK = 256
PIECE = 32
MESH = pl.DeviceIdType.MESH
LOG2E = 1.4426950408889634


def xor(a, b):
    total = 0
    for bit in (1, 2, 4):
        total = total + bit * (((a // bit) % 2 + (b // bit) % 2) % 2)
    return total


def kernel(
    q_hbm, k_hbm, v_hbm, seg_hbm, out_ref,
    q_ref, k_ref, v_ref, seg_ref, seg_col, sent, q_sem, in_sem, send_sem, recv_sem, ready,
):
    tokens, width = q_ref.shape
    chunk = tokens // HEADS
    pieces = chunk // PIECE
    half = HEADS // 2
    scale = WIDTH**-0.5 * LOG2E
    me = lax.axis_index("head")
    replica = lax.axis_index("dp")
    ones = 0
    for bit in range(16):
        ones = ones + (replica // 2**bit) % 2
    light = ones % 2
    flip = replica // (lax.axis_size("dp") // 2)
    place = me + flip * (HEADS - 1 - 2 * me)
    late = place // half

    def device(at):
        return at + flip * (HEADS - 1 - 2 * at)

    def target(step):
        last = step // (HEADS - 1)
        odd = (step % 2) * (1 - last)
        across = odd + 1 - (step + HEADS - 2) // (HEADS - 1)
        other = (step + 1) // 2 + half * (1 - late)
        near = half * late + xor(place % half, (step // 2) * (1 - last))
        return across * other + (1 - across) * near

    def q_copy(step):
        rows = pl.ds(pl.multiple_of(device(target(step)) * chunk, chunk), chunk)
        return pltpu.make_async_copy(q_hbm.at[rows], q_ref.at[rows], q_sem.at[step])

    def greet(at, semaphore):
        pl.semaphore_signal(
            semaphore, inc=1, device_id={"head": device(at)}, device_id_type=MESH
        )

    barrier = pltpu.get_barrier_semaphore()

    @pl.when(late == 0)
    def _():
        for at in range(half, HEADS):
            greet(at, barrier)

    @pl.when(place == half)
    def _():
        for at in range(half):
            greet(at, barrier)

    seg_copy = pltpu.make_async_copy(seg_hbm, seg_ref, in_sem.at[2])
    k_copy = pltpu.make_async_copy(k_hbm, k_ref, in_sem.at[0])
    v_copy = pltpu.make_async_copy(v_hbm, v_ref, in_sem.at[1])
    seg_copy.start()
    q_copy(0).start()
    k_copy.start()
    v_copy.start()
    for step in range(1, HEADS):
        q_copy(step).start()
    seg_copy.wait()
    for part in range(tokens // 128):
        row = seg_ref[0:1, part * 128 : (part + 1) * 128]
        seg_col[part * 128 : (part + 1) * 128, :] = jnp.broadcast_to(row, (128, 128)).T
    k_copy.wait()
    v_copy.wait()

    @pl.when(late == 0)
    def _():
        pl.semaphore_wait(barrier, 1)

    @pl.when(late == 1)
    def _():
        pl.semaphore_wait(barrier, half)
        for at in range(half):
            greet(at, ready.at[place - half])

    def admit(step):
        @pl.when(step == 2)
        def _():
            pl.semaphore_wait(ready.at[0], 1)

        @pl.when((late == 0) & (step % 2 == 1) & (step < HEADS - 1))
        def _():
            pl.semaphore_wait(ready.at[(step + 1) // 2], 1)

        @pl.when((place == half - 1) & (step == HEADS - 3))
        def _():
            for at in range(half, HEADS):
                greet(at, ready.at[0])

    def piece_copy(step, piece):
        partner = device(target(step))
        link = xor(me, partner) - 1
        source = pl.ds(pl.multiple_of(partner * chunk + piece * PIECE, PIECE), PIECE)
        return pltpu.make_async_remote_copy(
            src_ref=sent.at[source],
            dst_ref=out_ref.at[
                pl.ds(pl.multiple_of(piece * PIECE, PIECE), PIECE),
                pl.ds(pl.multiple_of(me * width, width), width),
            ],
            send_sem=send_sem.at[link, piece],
            recv_sem=recv_sem.at[link, piece],
            device_id={"head": partner},
            device_id_type=MESH,
        )

    def attend(first, key_first, blocks):
        keys = blocks * BLK
        rows = pl.ds(first, PIECE)
        window = pl.ds(key_first, keys)
        queries = jnp.concatenate(
            [q_ref[rows, g * WIDTH : (g + 1) * WIDTH] for g in range(GROUP)], axis=0
        )
        scores = lax.dot_general(
            queries, k_ref[window, :], (((1,), (1,)), ((), ())),
            preferred_element_type=jnp.float32,
        )
        own = seg_col[rows, :]
        own = jnp.concatenate([own] * (keys // 128), axis=1)
        key_seg = seg_ref[0:1, window]
        key_at = key_first + lax.broadcasted_iota(jnp.int32, (PIECE, keys), 1)
        own_at = first + lax.broadcasted_iota(jnp.int32, (PIECE, keys), 0)
        allowed = (own == key_seg) & (key_at <= own_at)
        bias = jnp.where(allowed, 0.0, -jnp.inf)
        scores = scores.reshape(GROUP, PIECE, keys) + bias[None]
        row_max = jnp.max(scores, axis=-1, keepdims=True)
        weights = jnp.exp2((scores - row_max) * scale)
        total = jnp.sum(weights, axis=-1, keepdims=True)
        mixed = jnp.dot(
            weights.astype(jnp.bfloat16).reshape(GROUP * PIECE, keys), v_ref[window, :],
            preferred_element_type=jnp.float32,
        )
        mixed = mixed.reshape(GROUP, PIECE, WIDTH) / total
        for g in range(GROUP):
            sent[rows, g * WIDTH : (g + 1) * WIDTH] = mixed[g].astype(jnp.bfloat16)

    def one_step(step, carry):
        partner = device(target(step))
        q_copy(step).wait()
        admit(step)
        block = partner // (BLK // chunk)
        blocks = light + (1 - light) * (block + 1)
        key_first = pl.multiple_of(light * block * BLK, BLK)

        def one_piece(piece, inner):
            first = pl.multiple_of(partner * chunk + piece * PIECE, PIECE)
            for count in range(1, tokens // BLK + 1):

                @pl.when(blocks == count)
                def _(count=count):
                    attend(first, key_first if count == 1 else 0, count)

            @pl.when(step < HEADS - 1)
            def _():
                piece_copy(step, piece).start()

            return inner

        return lax.fori_loop(0, pieces, one_piece, carry)

    lax.fori_loop(0, HEADS, one_step, 0)
    mine = pl.ds(pl.multiple_of(me * chunk, chunk), chunk)
    home = pltpu.make_async_copy(
        sent.at[mine],
        out_ref.at[:, pl.ds(pl.multiple_of(me * width, width), width)],
        in_sem.at[0],
    )
    home.start()
    home.wait()

    def finish(step, carry):
        def one_piece(piece, inner):
            copy = piece_copy(step, piece)
            copy.wait_send()
            copy.wait_recv()
            return inner

        return lax.fori_loop(0, pieces, one_piece, carry)

    lax.fori_loop(0, HEADS - 1, finish, 0)


def on_device(queries, keys, values, segments):
    tokens, width = queries.shape
    chunk = tokens // HEADS
    pieces = chunk // PIECE
    return pl.pallas_call(
        kernel,
        out_shape=pltpu.VMEM((chunk, HEADS * width), queries.dtype),
        in_specs=[pl.BlockSpec(memory_space=pl.ANY)] * 4,
        out_specs=pl.BlockSpec(memory_space=pltpu.VMEM),
        scratch_shapes=[
            pltpu.VMEM(queries.shape, queries.dtype),
            pltpu.VMEM(keys.shape, keys.dtype),
            pltpu.VMEM(values.shape, values.dtype),
            pltpu.VMEM(segments.shape, segments.dtype),
            pltpu.VMEM((tokens, 128), jnp.int32),
            pltpu.VMEM(queries.shape, queries.dtype),
            pltpu.SemaphoreType.DMA((HEADS,)),
            pltpu.SemaphoreType.DMA((3,)),
            pltpu.SemaphoreType.DMA((HEADS - 1, pieces)),
            pltpu.SemaphoreType.DMA((HEADS - 1, pieces)),
            pltpu.SemaphoreType.REGULAR((HEADS // 2,)),
        ],
        compiler_params=pltpu.CompilerParams(
            collective_id=0, has_side_effects=True, vmem_limit_bytes=60 * 2**20
        ),
        cost_estimate=pl.CostEstimate(
            flops=4 * tokens * width * tokens, bytes_accessed=5 * 2**20,
            transcendentals=tokens * GROUP * tokens,
        ),
    )(queries, keys, values, segments)


def solution(mesh):
    placed = (P("dp", "head"), P("dp", "head"), P("dp", "head"), P("dp", None))
    return jax.shard_map(
        on_device, mesh=mesh, in_specs=placed, out_specs=P(("dp", "head"), None), check_vma=False
    )
```

```python
import jax
import jax.numpy as jnp
from jax import lax
from jax.experimental import pallas as pl
from jax.experimental.pallas import tpu as pltpu
from jax.sharding import PartitionSpec as P

HEADS = 8
WIDTH = 128
GROUP = 8
BLK = 256
PIECE = 32
MESH = pl.DeviceIdType.MESH
LOG2E = 1.4426950408889634
PACKED = 3
TOGETHER = (4, 2, 4)


def keys_of(piece):
    return (piece + 1) * PIECE


def xor(a, b):
    total = 0
    for bit in (1, 2, 4):
        total = total + bit * (((a // bit) % 2 + (b // bit) % 2) % 2)
    return total


def kernel(
    q_hbm, k_hbm, v_hbm, seg_hbm, out_ref,
    q_ref, k_ref, v_ref, seg_ref, seg_col, sent, v_came, spread_0, spread_1, spread_2,
    q_sem, in_sem, send_sem, recv_sem, v_send_sem, v_recv_sem, ready,
):
    tokens, width = q_ref.shape
    chunk = tokens // HEADS
    pieces = chunk // PIECE
    half = HEADS // 2
    spread = (spread_0, spread_1, spread_2)
    scale = WIDTH**-0.5 * LOG2E
    me = lax.axis_index("head")
    replica = lax.axis_index("dp")
    ones = 0
    for bit in range(16):
        ones = ones + (replica // 2**bit) % 2
    light = ones % 2

    def narrow(at):
        even = 1 - at % (BLK // chunk)
        first = 1 - (at + HEADS - 1) // HEADS
        return light * even + (1 - light) * first

    flip = replica // (lax.axis_size("dp") // 2)
    place = me + flip * (HEADS - 1 - 2 * me)
    late = place // half

    def device(at):
        return at + flip * (HEADS - 1 - 2 * at)

    def target(step):
        last = step // (HEADS - 1)
        odd = (step % 2) * (1 - last)
        across = odd + 1 - (step + HEADS - 2) // (HEADS - 1)
        other = (step + 1) // 2 + half * (1 - late)
        near = half * late + xor(place % half, (step // 2) * (1 - last))
        return across * other + (1 - across) * near

    def q_copy(step):
        rows = pl.ds(pl.multiple_of(device(target(step)) * chunk, chunk), chunk)
        return pltpu.make_async_copy(q_hbm.at[rows], q_ref.at[rows], q_sem.at[step])

    def greet(at, semaphore):
        pl.semaphore_signal(
            semaphore, inc=1, device_id={"head": device(at)}, device_id_type=MESH
        )

    barrier = pltpu.get_barrier_semaphore()

    @pl.when(late == 0)
    def _():
        for at in range(half, HEADS):
            greet(at, barrier)

    @pl.when(place == half)
    def _():
        for at in range(half):
            greet(at, barrier)

    seg_copy = pltpu.make_async_copy(seg_hbm, seg_ref, in_sem.at[2])
    k_copy = pltpu.make_async_copy(k_hbm, k_ref, in_sem.at[0])
    v_copy = pltpu.make_async_copy(v_hbm, v_ref, in_sem.at[1])
    seg_copy.start()
    q_copy(0).start()
    k_copy.start()
    v_copy.start()
    for step in range(1, HEADS):
        q_copy(step).start()
    seg_copy.wait()
    for part in range(tokens // 128):
        row = seg_ref[0:1, part * 128 : (part + 1) * 128]
        seg_col[part * 128 : (part + 1) * 128, :] = jnp.broadcast_to(row, (128, 128)).T
    for piece in range(PACKED):
        keys = keys_of(piece)
        spread[piece][...] = jnp.zeros_like(spread[piece])
        row = lax.broadcasted_iota(jnp.int32, (keys, WIDTH), 0)
        column = lax.broadcasted_iota(jnp.int32, (keys, WIDTH), 1)
        unit = jnp.where(row == column, 1.0, 0.0).astype(jnp.bfloat16)
        for g in range(TOGETHER[piece]):
            spread[piece][g * keys : (g + 1) * keys, g * WIDTH : (g + 1) * WIDTH] = unit
    k_copy.wait()
    v_copy.wait()

    @pl.when(late == 0)
    def _():
        pl.semaphore_wait(barrier, 1)

    @pl.when(late == 1)
    def _():
        pl.semaphore_wait(barrier, half)
        for at in range(half):
            greet(at, ready.at[place - half])

    def admit(step):
        @pl.when(step == 2)
        def _():
            pl.semaphore_wait(ready.at[0], 1)

        @pl.when((late == 0) & (step % 2 == 1) & (step < HEADS - 1))
        def _():
            pl.semaphore_wait(ready.at[(step + 1) // 2], 1)

        @pl.when((place == half - 1) & (step == HEADS - 3))
        def _():
            for at in range(half, HEADS):
                greet(at, ready.at[0])

    def piece_copy(step, piece, columns):
        partner = device(target(step))
        link = xor(me, partner) - 1
        source = pl.ds(pl.multiple_of(partner * chunk + piece * PIECE, PIECE), PIECE)
        return pltpu.make_async_remote_copy(
            src_ref=sent.at[source, pl.ds(0, columns)],
            dst_ref=out_ref.at[
                pl.ds(pl.multiple_of(piece * PIECE, PIECE), PIECE),
                pl.ds(pl.multiple_of(me * width, width), columns),
            ],
            send_sem=send_sem.at[link, piece],
            recv_sem=recv_sem.at[link, piece],
            device_id={"head": partner},
            device_id_type=MESH,
        )

    def value_copy(step):
        partner = device(target(step))
        link = xor(me, partner) - 1
        rows = keys_of(PACKED - 1)
        return pltpu.make_async_remote_copy(
            src_ref=v_ref.at[pl.ds(pl.multiple_of(partner * chunk, chunk), rows)],
            dst_ref=v_came.at[link],
            send_sem=v_send_sem.at[link],
            recv_sem=v_recv_sem.at[link],
            device_id={"head": partner},
            device_id_type=MESH,
        )

    def each_form(is_narrow, piece, act):
        for number in range(PACKED):

            @pl.when((is_narrow == 1) & (piece == number))
            def _(number=number):
                act(keys_of(number) * GROUP, number)

        @pl.when((is_narrow == 0) | (piece >= PACKED))
        def _():
            act(width, None)

    def weigh(first, key_first, keys):
        rows = pl.ds(first, PIECE)
        queries = jnp.concatenate(
            [q_ref[rows, g * WIDTH : (g + 1) * WIDTH] for g in range(GROUP)], axis=0
        )
        scores = lax.dot_general(
            queries, k_ref[pl.ds(key_first, keys), :], (((1,), (1,)), ((), ())),
            preferred_element_type=jnp.float32,
        )
        own = seg_col[rows, :]
        own = jnp.concatenate([own] * (keys // 128), axis=1)
        key_seg = seg_ref[0:1, pl.ds(key_first, keys)]
        key_at = key_first + lax.broadcasted_iota(jnp.int32, (PIECE, keys), 1)
        own_at = first + lax.broadcasted_iota(jnp.int32, (PIECE, keys), 0)
        allowed = (own == key_seg) & (key_at <= own_at)
        bias = jnp.where(allowed, 0.0, -jnp.inf)
        scores = scores.reshape(GROUP, PIECE, keys) + bias[None]
        row_max = jnp.max(scores, axis=-1, keepdims=True)
        return jnp.exp2((scores - row_max) * scale)

    def attend(first, key_first, blocks):
        keys = blocks * BLK
        weights = weigh(first, key_first, keys)
        total = jnp.sum(weights, axis=-1, keepdims=True)
        mixed = jnp.dot(
            weights.astype(jnp.bfloat16).reshape(GROUP * PIECE, keys),
            v_ref[pl.ds(key_first, keys), :],
            preferred_element_type=jnp.float32,
        )
        mixed = mixed.reshape(GROUP, PIECE, WIDTH) / total
        for g in range(GROUP):
            sent[pl.ds(first, PIECE), g * WIDTH : (g + 1) * WIDTH] = mixed[g].astype(jnp.bfloat16)

    def pack(first, key_first, number):
        weights = weigh(first, key_first, chunk).astype(jnp.bfloat16)
        together, keys = TOGETHER[number], keys_of(number)
        for start in range(0, GROUP, together):
            wide = jnp.concatenate([weights[start + g] for g in range(together)], axis=1)
            dense = lax.dot_general(
                wide, spread[number][...], (((1,), (1,)), ((), ())),
                preferred_element_type=jnp.float32,
            )
            sent[pl.ds(first, PIECE), start * keys : (start + together) * keys] = dense.astype(
                jnp.bfloat16
            )

    def expand(source, link):
        at = pl.multiple_of(source * width, width)
        came = v_came[link]
        came = jnp.concatenate(
            [came, jnp.zeros((WIDTH - came.shape[0], WIDTH), came.dtype)], axis=0
        )
        done = []
        for number in range(PACKED):
            together, keys = TOGETHER[number], keys_of(number)
            rows = pl.ds(number * PIECE, PIECE)
            wide = [
                jnp.dot(
                    out_ref[rows, pl.ds(pl.multiple_of(at + start * keys, 128), together * keys)],
                    spread[number][...], preferred_element_type=jnp.float32,
                )
                for start in range(0, GROUP, together)
            ]
            weights = jnp.concatenate(
                [w[:, g * WIDTH : (g + 1) * WIDTH] for w in wide for g in range(together)], axis=0
            )
            total = jnp.sum(weights, axis=-1, keepdims=True)
            mixed = jnp.dot(
                weights.astype(jnp.bfloat16), came, preferred_element_type=jnp.float32
            )
            done.append((mixed * (1.0 / total)).astype(jnp.bfloat16))
        for number in range(PACKED):
            for g in range(GROUP):
                out_ref[
                    number * PIECE : (number + 1) * PIECE,
                    pl.ds(pl.multiple_of(at + g * WIDTH, WIDTH), WIDTH),
                ] = done[number][g * PIECE : (g + 1) * PIECE]

    def one_step(step, carry):
        partner = device(target(step))
        q_copy(step).wait()
        admit(step)
        block = partner // (BLK // chunk)
        blocks = light + (1 - light) * (block + 1)
        key_first = pl.multiple_of(light * block * BLK, BLK)

        away = 1 - step // (HEADS - 1)
        is_narrow = narrow(partner) * away

        @pl.when(is_narrow == 1)
        def _():
            value_copy(step).start()

        def one_piece(piece, inner):
            first = pl.multiple_of(partner * chunk + piece * PIECE, PIECE)

            def form(columns, number):
                if number is None:
                    for count in range(1, tokens // BLK + 1):

                        @pl.when(blocks == count)
                        def _(count=count):
                            attend(first, key_first if count == 1 else 0, count)
                else:
                    pack(first, key_first, number)

                @pl.when(away == 1)
                def _():
                    piece_copy(step, piece, columns).start()

            each_form(is_narrow, piece, form)
            return inner

        return lax.fori_loop(0, pieces, one_piece, carry)

    lax.fori_loop(0, HEADS, one_step, 0)
    mine = pl.ds(pl.multiple_of(me * chunk, chunk), chunk)
    home = pltpu.make_async_copy(
        sent.at[mine],
        out_ref.at[:, pl.ds(pl.multiple_of(me * width, width), width)],
        in_sem.at[0],
    )
    home.start()
    home.wait()

    def unpack(place_in_order, carry):
        near = place_in_order // half
        step = (1 - near) * (place_in_order * 2 - (place_in_order + 3) // half) + near * 2 * (
            place_in_order - half + 1
        )
        partner = device(target(step))
        value_copy(step).wait_recv()
        for number in range(PACKED):
            piece_copy(step, number, keys_of(number) * GROUP).wait_recv()
        expand(partner, xor(me, partner) - 1)
        return carry

    @pl.when(narrow(me) == 1)
    def _():
        lax.fori_loop(0, HEADS - 1, unpack, 0)

    def arrive(step, carry):
        def one_piece(piece, inner):
            piece_copy(step, piece, width).wait_recv()
            return inner

        return lax.fori_loop(narrow(me) * PACKED, pieces, one_piece, carry)

    lax.fori_loop(0, HEADS - 1, arrive, 0)

    def leave(step, carry):
        is_narrow = narrow(device(target(step)))

        @pl.when(is_narrow == 1)
        def _():
            value_copy(step).wait_send()

        def one_piece(piece, inner):
            def form(columns, number):
                piece_copy(step, piece, columns).wait_send()

            each_form(is_narrow, piece, form)
            return inner

        return lax.fori_loop(0, pieces, one_piece, carry)

    lax.fori_loop(0, HEADS - 1, leave, 0)


def on_device(queries, keys, values, segments):
    tokens, width = queries.shape
    chunk = tokens // HEADS
    pieces = chunk // PIECE
    return pl.pallas_call(
        kernel,
        out_shape=pltpu.VMEM((chunk, HEADS * width), queries.dtype),
        in_specs=[pl.BlockSpec(memory_space=pl.ANY)] * 4,
        out_specs=pl.BlockSpec(memory_space=pltpu.VMEM),
        scratch_shapes=[
            pltpu.VMEM(queries.shape, queries.dtype),
            pltpu.VMEM(keys.shape, keys.dtype),
            pltpu.VMEM(values.shape, values.dtype),
            pltpu.VMEM(segments.shape, segments.dtype),
            pltpu.VMEM((tokens, 128), jnp.int32),
            pltpu.VMEM(queries.shape, queries.dtype),
            pltpu.VMEM((HEADS - 1, keys_of(PACKED - 1), WIDTH), values.dtype),
            *[
                pltpu.VMEM((TOGETHER[p] * keys_of(p), TOGETHER[p] * WIDTH), queries.dtype)
                for p in range(PACKED)
            ],
            pltpu.SemaphoreType.DMA((HEADS,)),
            pltpu.SemaphoreType.DMA((3,)),
            pltpu.SemaphoreType.DMA((HEADS - 1, pieces)),
            pltpu.SemaphoreType.DMA((HEADS - 1, pieces)),
            pltpu.SemaphoreType.DMA((HEADS - 1,)),
            pltpu.SemaphoreType.DMA((HEADS - 1,)),
            pltpu.SemaphoreType.REGULAR((HEADS // 2,)),
        ],
        compiler_params=pltpu.CompilerParams(
            collective_id=0, has_side_effects=True, vmem_limit_bytes=60 * 2**20
        ),
        cost_estimate=pl.CostEstimate(
            flops=4 * tokens * width * tokens, bytes_accessed=5 * 2**20,
            transcendentals=tokens * GROUP * tokens,
        ),
    )(queries, keys, values, segments)


def solution(mesh):
    placed = (P("dp", "head"), P("dp", "head"), P("dp", "head"), P("dp", None))
    return jax.shard_map(
        on_device, mesh=mesh, in_specs=placed, out_specs=P(("dp", "head"), None), check_vma=False
    )
```

```python
import jax
import jax.numpy as jnp
from jax import lax
from jax.experimental import pallas as pl
from jax.experimental.pallas import tpu as pltpu
from jax.sharding import PartitionSpec as P

HEADS = 8
WIDTH = 128
GROUP = 8
BLK = 256
PIECE = 32
MESH = pl.DeviceIdType.MESH
LOG2E = 1.4426950408889634
PACKED = 3
ORDER = (0, -3, 1, -2, 2, -1, 3)
EARLY = ((0, 3, 2, 1), (3, 2, 1, 0))
FIRST_NEAR = min(step for step, turn in enumerate(ORDER) if turn < 0)
TOGETHER = (4, 2, 4)


def keys_of(piece):
    return (piece + 1) * PIECE


def pick(step, values):
    chosen = values[-1]
    for at in range(len(values) - 2, -1, -1):
        chosen = jnp.where(step == at, values[at], chosen)
    return chosen


def kernel(
    q_hbm, k_hbm, v_hbm, seg_hbm, out_ref,
    q_ref, k_ref, v_ref, seg_ref, seg_col, sent, v_came, spread_0, spread_1, spread_2,
    q_sem, in_sem, send_sem, wide_sem, packed_sem, ready,
):
    tokens, width = q_ref.shape
    chunk = tokens // HEADS
    pieces = chunk // PIECE
    half = HEADS // 2
    spread = (spread_0, spread_1, spread_2)
    scale = WIDTH**-0.5 * LOG2E
    me = lax.axis_index("head")
    replica = lax.axis_index("dp")
    replicas = lax.axis_size("dp")
    ones = 0
    for bit in range((replicas - 1).bit_length()):
        ones = ones + lax.rem(lax.div(replica, 2**bit), 2)
    light = lax.rem(ones, 2)

    def narrow(at):
        even = 1 - lax.rem(at, BLK // chunk)
        first = 1 - lax.div(at + HEADS - 1, HEADS)
        return light * even + (1 - light) * first

    flip = lax.div(replica, replicas // 2)
    place = me + flip * (HEADS - 1 - 2 * me)
    late = lax.div(place, half)
    within = place - half * late
    low = lax.rem(within, 2)
    high = lax.div(within, 2)

    def mixed_with(i):
        return (1 - low if i % 2 else low) + 2 * (1 - high if i // 2 else high)

    def device(at):
        return at + flip * (HEADS - 1 - 2 * at)

    kind = (1 - late) * (1 + flip)
    partners, links = [], []
    for turn in ORDER:
        if turn >= 0:
            orders = (turn, EARLY[0][turn], EARLY[1][turn])
            partners.append(device(pick(kind, orders) + half * (1 - late)))
            links.append(half - 1 + pick(kind, [mixed_with(at) for at in orders]))
        else:
            partners.append(device(half * late + mixed_with(-turn)))
            links.append(-turn - 1)
    partners.append(me)
    links.append(0)
    narrows = [narrow(at) for at in partners]
    narrow_here = narrow(me)

    def q_copy(step, partner):
        rows = pl.ds(pl.multiple_of(partner * chunk, chunk), chunk)
        return pltpu.make_async_copy(q_hbm.at[rows], q_ref.at[rows], q_sem.at[step])

    def greet(at, semaphore):
        pl.semaphore_signal(
            semaphore, inc=1, device_id={"head": device(at)}, device_id_type=MESH
        )

    barrier = pltpu.get_barrier_semaphore()

    @pl.when(late == 0)
    def _():
        for at in range(half, HEADS):
            greet(at, barrier)

    @pl.when(place == half)
    def _():
        for at in range(half):
            greet(at, barrier)

    seg_copy = pltpu.make_async_copy(seg_hbm, seg_ref, in_sem.at[2])
    k_copy = pltpu.make_async_copy(k_hbm, k_ref, in_sem.at[0])
    v_copy = pltpu.make_async_copy(v_hbm, v_ref, in_sem.at[1])
    seg_copy.start()
    q_copy(0, partners[0]).start()
    k_copy.start()
    v_copy.start()
    for step in range(1, HEADS):
        q_copy(step, partners[step]).start()
    seg_copy.wait()
    for part in range(tokens // 128):
        row = seg_ref[0:1, part * 128 : (part + 1) * 128]
        seg_col[part * 128 : (part + 1) * 128, :] = jnp.broadcast_to(row, (128, 128)).T
    for piece in range(PACKED):
        keys = keys_of(piece)
        spread[piece][...] = jnp.zeros_like(spread[piece])
        row = lax.broadcasted_iota(jnp.int32, (keys, WIDTH), 0)
        column = lax.broadcasted_iota(jnp.int32, (keys, WIDTH), 1)
        unit = jnp.where(row == column, 1.0, 0.0).astype(jnp.bfloat16)
        for g in range(TOGETHER[piece]):
            spread[piece][g * keys : (g + 1) * keys, g * WIDTH : (g + 1) * WIDTH] = unit
    k_copy.wait()
    v_copy.wait()

    @pl.when(late == 0)
    def _():
        pl.semaphore_wait(barrier, 1)

    @pl.when(late == 1)
    def _():
        pl.semaphore_wait(barrier, half)
        for at in range(half):
            greet(at, ready.at[place - half])

    def admit(step):
        @pl.when((late == 0) & (step == 1 - flip))
        def _():
            for at in range(half):
                pl.semaphore_wait(ready.at[at], 1)

        @pl.when((place == half - 1) & (step == 1 - flip))
        def _():
            for at in range(half, HEADS):
                greet(at, ready.at[0])

        @pl.when((late == 1) & (step == FIRST_NEAR))
        def _():
            pl.semaphore_wait(ready.at[0], 1)

    def piece_copy(partner, link, piece, columns, came):
        source = pl.ds(pl.multiple_of(partner * chunk + piece * PIECE, PIECE), PIECE)
        return pltpu.make_async_remote_copy(
            src_ref=sent.at[source, pl.ds(0, columns)],
            dst_ref=out_ref.at[
                pl.ds(pl.multiple_of(piece * PIECE, PIECE), PIECE),
                pl.ds(pl.multiple_of(me * width, width), columns),
            ],
            send_sem=send_sem.at[link],
            recv_sem=came,
            device_id={"head": partner},
            device_id_type=MESH,
        )

    def value_copy(partner, link):
        rows = keys_of(PACKED - 1)
        return pltpu.make_async_remote_copy(
            src_ref=v_ref.at[pl.ds(pl.multiple_of(partner * chunk, chunk), rows)],
            dst_ref=v_came.at[link],
            send_sem=send_sem.at[link],
            recv_sem=packed_sem.at[link],
            device_id={"head": partner},
            device_id_type=MESH,
        )

    def wait_bytes(semaphore, ref):
        pltpu.make_async_copy(ref, ref, semaphore).wait()

    def each_form(is_narrow, piece, act):
        for number in range(PACKED):

            @pl.when((is_narrow == 1) & (piece == number))
            def _(number=number):
                act(keys_of(number) * GROUP, number)

        @pl.when((is_narrow == 0) | (piece >= PACKED))
        def _():
            act(width, None)

    def weigh(first, key_first, keys):
        rows = pl.ds(first, PIECE)
        queries = jnp.concatenate(
            [q_ref[rows, g * WIDTH : (g + 1) * WIDTH] for g in range(GROUP)], axis=0
        )
        scores = lax.dot_general(
            queries, k_ref[pl.ds(key_first, keys), :], (((1,), (1,)), ((), ())),
            preferred_element_type=jnp.float32,
        )
        own = seg_col[rows, :]
        own = jnp.concatenate([own] * (keys // 128), axis=1)
        key_seg = seg_ref[0:1, pl.ds(key_first, keys)]
        key_at = key_first + lax.broadcasted_iota(jnp.int32, (PIECE, keys), 1)
        own_at = first + lax.broadcasted_iota(jnp.int32, (PIECE, keys), 0)
        allowed = (own == key_seg) & (key_at <= own_at)
        bias = jnp.where(allowed, 0.0, -jnp.inf)
        scores = scores.reshape(GROUP, PIECE, keys) + bias[None]
        row_max = jnp.max(scores, axis=-1, keepdims=True)
        return jnp.exp2((scores - row_max) * scale)

    def attend(first, key_first, blocks):
        keys = blocks * BLK
        weights = weigh(first, key_first, keys)
        total = jnp.sum(weights, axis=-1, keepdims=True)
        mixed = jnp.dot(
            weights.astype(jnp.bfloat16).reshape(GROUP * PIECE, keys),
            v_ref[pl.ds(key_first, keys), :],
            preferred_element_type=jnp.float32,
        )
        mixed = mixed.reshape(GROUP, PIECE, WIDTH) / total
        for g in range(GROUP):
            sent[pl.ds(first, PIECE), g * WIDTH : (g + 1) * WIDTH] = mixed[g].astype(jnp.bfloat16)

    def pack(first, key_first, number):
        weights = weigh(first, key_first, chunk).astype(jnp.bfloat16)
        together, keys = TOGETHER[number], keys_of(number)
        for start in range(0, GROUP, together):
            wide = jnp.concatenate([weights[start + g] for g in range(together)], axis=1)
            dense = lax.dot_general(
                wide, spread[number][...], (((1,), (1,)), ((), ())),
                preferred_element_type=jnp.float32,
            )
            sent[pl.ds(first, PIECE), start * keys : (start + together) * keys] = dense.astype(
                jnp.bfloat16
            )

    def expand(source, link):
        at = pl.multiple_of(source * width, width)
        came = v_came[link]
        came = jnp.concatenate(
            [came, jnp.zeros((WIDTH - came.shape[0], WIDTH), came.dtype)], axis=0
        )
        done = []
        for number in range(PACKED):
            together, keys = TOGETHER[number], keys_of(number)
            rows = pl.ds(number * PIECE, PIECE)
            wide = [
                jnp.dot(
                    out_ref[rows, pl.ds(pl.multiple_of(at + start * keys, 128), together * keys)],
                    spread[number][...], preferred_element_type=jnp.float32,
                )
                for start in range(0, GROUP, together)
            ]
            weights = jnp.concatenate(
                [w[:, g * WIDTH : (g + 1) * WIDTH] for w in wide for g in range(together)], axis=0
            )
            total = jnp.sum(weights, axis=-1, keepdims=True)
            mixed = jnp.dot(
                weights.astype(jnp.bfloat16), came, preferred_element_type=jnp.float32
            )
            done.append((mixed * (1.0 / total)).astype(jnp.bfloat16))
        for number in range(PACKED):
            for g in range(GROUP):
                out_ref[
                    number * PIECE : (number + 1) * PIECE,
                    pl.ds(pl.multiple_of(at + g * WIDTH, WIDTH), WIDTH),
                ] = done[number][g * PIECE : (g + 1) * PIECE]

    def one_step(step, carry):
        partner, link = pick(step, partners), pick(step, links)
        q_copy(step, partner).wait()
        admit(step)
        block = lax.div(partner, BLK // chunk)
        blocks = light + (1 - light) * (block + 1)
        key_first = pl.multiple_of(light * block * BLK, BLK)
        is_narrow = pick(step, narrows[:-1] + [0])

        @pl.when(is_narrow == 1)
        def _():
            value_copy(partner, link).start()

        def one_piece(piece, inner):
            first = pl.multiple_of(partner * chunk + piece * PIECE, PIECE)

            def form(columns, number):
                if number is None:
                    for count in range(1, tokens // BLK + 1):

                        @pl.when(blocks == count)
                        def _(count=count):
                            attend(first, key_first if count == 1 else 0, count)
                else:
                    pack(first, key_first, number)

                @pl.when(step < HEADS - 1)
                def _():
                    came = wide_sem.at[0] if number is None else packed_sem.at[link]
                    piece_copy(partner, link, piece, columns, came).start()

            each_form(is_narrow, piece, form)
            return inner

        return lax.fori_loop(0, pieces, one_piece, carry)

    lax.fori_loop(0, HEADS, one_step, 0)
    mine = pl.ds(pl.multiple_of(me * chunk, chunk), chunk)
    home = pltpu.make_async_copy(
        sent.at[mine],
        out_ref.at[:, pl.ds(pl.multiple_of(me * width, width), width)],
        in_sem.at[0],
    )
    home.start()
    home.wait()

    weight_rows = sum(keys_of(p) * GROUP * PIECE for p in range(PACKED)) // WIDTH
    packed_rows = weight_rows + keys_of(PACKED - 1)
    wide_rows = PIECE * width // WIDTH

    def unpack(at, carry):
        link = pick(at, links)
        wait_bytes(packed_sem.at[link], k_ref.at[pl.ds(0, packed_rows)])
        expand(pick(at, partners), link)
        return carry

    @pl.when(narrow_here == 1)
    def _():
        lax.fori_loop(0, HEADS - 1, unpack, 0)

    for step in range(HEADS - 1):

        @pl.when(narrows[step] == 1)
        def _(step=step):
            left = packed_rows + (pieces - PACKED) * wide_rows
            wait_bytes(send_sem.at[links[step]], k_ref.at[pl.ds(0, left)])

        @pl.when(narrows[step] == 0)
        def _(step=step):
            wait_bytes(send_sem.at[links[step]], k_ref.at[pl.ds(0, pieces * wide_rows)])

    others = pl.ds(0, (HEADS - 1) * width)

    @pl.when(narrow_here == 1)
    def _():
        wait_bytes(wide_sem.at[0], out_ref.at[pl.ds(0, (pieces - PACKED) * PIECE), others])

    @pl.when(narrow_here == 0)
    def _():
        wait_bytes(wide_sem.at[0], out_ref.at[:, others])


def on_device(queries, keys, values, segments):
    tokens, width = queries.shape
    chunk = tokens // HEADS
    return pl.pallas_call(
        kernel,
        out_shape=pltpu.VMEM((chunk, HEADS * width), queries.dtype),
        in_specs=[pl.BlockSpec(memory_space=pl.ANY)] * 4,
        out_specs=pl.BlockSpec(memory_space=pltpu.VMEM),
        scratch_shapes=[
            pltpu.VMEM(queries.shape, queries.dtype),
            pltpu.VMEM(keys.shape, keys.dtype),
            pltpu.VMEM(values.shape, values.dtype),
            pltpu.VMEM(segments.shape, segments.dtype),
            pltpu.VMEM((tokens, 128), jnp.int32),
            pltpu.VMEM(queries.shape, queries.dtype),
            pltpu.VMEM((HEADS - 1, keys_of(PACKED - 1), WIDTH), values.dtype),
            *[
                pltpu.VMEM((TOGETHER[p] * keys_of(p), TOGETHER[p] * WIDTH), queries.dtype)
                for p in range(PACKED)
            ],
            pltpu.SemaphoreType.DMA((HEADS,)),
            pltpu.SemaphoreType.DMA((3,)),
            pltpu.SemaphoreType.DMA((HEADS - 1,)),
            pltpu.SemaphoreType.DMA((1,)),
            pltpu.SemaphoreType.DMA((HEADS - 1,)),
            pltpu.SemaphoreType.REGULAR((HEADS // 2,)),
        ],
        compiler_params=pltpu.CompilerParams(
            collective_id=0, has_side_effects=True, vmem_limit_bytes=60 * 2**20
        ),
        cost_estimate=pl.CostEstimate(
            flops=4 * tokens * width * tokens, bytes_accessed=5 * 2**20,
            transcendentals=tokens * GROUP * tokens,
        ),
    )(queries, keys, values, segments)


def solution(mesh):
    placed = (P("dp", "head"), P("dp", "head"), P("dp", "head"), P("dp", None))
    return jax.shard_map(
        on_device, mesh=mesh, in_specs=placed, out_specs=P(("dp", "head"), None), check_vma=False
    )
```

```python
import jax
import jax.numpy as jnp
from jax import lax
from jax.experimental import pallas as pl
from jax.experimental.pallas import tpu as pltpu
from jax.sharding import PartitionSpec as P

HEADS = 8
WIDTH = 128
GROUP = 8
BLK = 256
PIECE = 32
MESH = pl.DeviceIdType.MESH
LOG2E = 1.4426950408889634
PACKED = 3
ORDER = (0, -3, 1, -2, 2, -1, 3)
EARLY = ((0, 3, 2, 1), (3, 2, 1, 0))
FIRST_NEAR = min(step for step, turn in enumerate(ORDER) if turn < 0)
TOGETHER = (4, 2, 4)


def keys_of(piece):
    return (piece + 1) * PIECE


def pick(step, values):
    chosen = values[-1]
    for at in range(len(values) - 2, -1, -1):
        chosen = jnp.where(step == at, values[at], chosen)
    return chosen


def kernel(
    q_hbm, k_hbm, v_hbm, seg_hbm, out_ref,
    q_ref, k_ref, v_ref, seg_ref, seg_col, sent, v_came, spread_0, spread_1, spread_2,
    q_sem, in_sem, send_sem, wide_sem, packed_sem, ready,
):
    tokens, width = q_ref.shape
    chunk = tokens // HEADS
    pieces = chunk // PIECE
    half = HEADS // 2
    spread = (spread_0, spread_1, spread_2)
    scale = WIDTH**-0.5 * LOG2E
    me = lax.axis_index("head")
    replica = lax.axis_index("dp")
    replicas = lax.axis_size("dp")
    ones = 0
    for bit in range((replicas - 1).bit_length()):
        ones = ones + lax.rem(lax.div(replica, 2**bit), 2)
    light = lax.rem(ones, 2)

    def narrow(at):
        even = 1 - lax.rem(at, BLK // chunk)
        first = 1 - lax.div(at + HEADS - 1, HEADS)
        return light * even + (1 - light) * first

    flip = lax.div(replica, replicas // 2)
    place = me + flip * (HEADS - 1 - 2 * me)
    late = lax.div(place, half)
    within = place - half * late
    low = lax.rem(within, 2)
    high = lax.div(within, 2)

    def mixed_with(i):
        return (1 - low if i % 2 else low) + 2 * (1 - high if i // 2 else high)

    def device(at):
        return at + flip * (HEADS - 1 - 2 * at)

    kind = (1 - late) * (1 + flip)
    partners, links = [], []
    for turn in ORDER:
        if turn >= 0:
            orders = (turn, EARLY[0][turn], EARLY[1][turn])
            partners.append(device(pick(kind, orders) + half * (1 - late)))
            links.append(half - 1 + pick(kind, [mixed_with(at) for at in orders]))
        else:
            partners.append(device(half * late + mixed_with(-turn)))
            links.append(-turn - 1)
    partners.append(me)
    links.append(0)
    narrows = [narrow(at) for at in partners]
    narrow_here = narrow(me)

    def q_copy(step, partner):
        rows = pl.ds(pl.multiple_of(partner * chunk, chunk), chunk)
        return pltpu.make_async_copy(q_hbm.at[rows], q_ref.at[rows], q_sem.at[step])

    def greet(at, semaphore):
        pl.semaphore_signal(
            semaphore, inc=1, device_id={"head": device(at)}, device_id_type=MESH
        )

    barrier = pltpu.get_barrier_semaphore()

    @pl.when(late == 0)
    def _():
        for at in range(half, HEADS):
            greet(at, barrier)

    @pl.when(place == half)
    def _():
        for at in range(half):
            greet(at, barrier)

    seg_copy = pltpu.make_async_copy(seg_hbm, seg_ref, in_sem.at[2])
    k_copy = pltpu.make_async_copy(k_hbm, k_ref, in_sem.at[0])
    v_copy = pltpu.make_async_copy(v_hbm, v_ref, in_sem.at[1])
    seg_copy.start()
    q_copy(0, partners[0]).start()
    k_copy.start()
    v_copy.start()
    for step in range(1, HEADS):
        q_copy(step, partners[step]).start()
    @pl.when(late == 1)
    def _():
        pl.semaphore_wait(barrier, half)
        for at in range(half):
            greet(at, ready.at[place - half])

    seg_copy.wait()
    for part in range(tokens // 128):
        row = seg_ref[0:1, part * 128 : (part + 1) * 128]
        seg_col[part * 128 : (part + 1) * 128, :] = jnp.broadcast_to(row, (128, 128)).T
    for piece in range(PACKED):
        keys = keys_of(piece)
        spread[piece][...] = jnp.zeros_like(spread[piece])
        row = lax.broadcasted_iota(jnp.int32, (keys, WIDTH), 0)
        column = lax.broadcasted_iota(jnp.int32, (keys, WIDTH), 1)
        unit = jnp.where(row == column, 1.0, 0.0).astype(jnp.bfloat16)
        for g in range(TOGETHER[piece]):
            spread[piece][g * keys : (g + 1) * keys, g * WIDTH : (g + 1) * WIDTH] = unit
    k_copy.wait()
    v_copy.wait()

    def admit(step):
        @pl.when((late == 0) & (step == 0))
        def _():
            pl.semaphore_wait(barrier, 1)

        @pl.when((late == 0) & (step == 1 - flip))
        def _():
            for at in range(half):
                pl.semaphore_wait(ready.at[at], 1)

        @pl.when((place == half - 1) & (step == 1 - flip))
        def _():
            for at in range(half, HEADS):
                greet(at, ready.at[0])

        @pl.when((late == 1) & (step == FIRST_NEAR))
        def _():
            pl.semaphore_wait(ready.at[0], 1)

    def piece_copy(partner, link, piece, columns, came):
        source = pl.ds(pl.multiple_of(partner * chunk + piece * PIECE, PIECE), PIECE)
        return pltpu.make_async_remote_copy(
            src_ref=sent.at[source, pl.ds(0, columns)],
            dst_ref=out_ref.at[
                pl.ds(pl.multiple_of(piece * PIECE, PIECE), PIECE),
                pl.ds(pl.multiple_of(me * width, width), columns),
            ],
            send_sem=send_sem.at[link],
            recv_sem=came,
            device_id={"head": partner},
            device_id_type=MESH,
        )

    def value_copy(partner, link):
        rows = keys_of(PACKED - 1)
        return pltpu.make_async_remote_copy(
            src_ref=v_ref.at[pl.ds(pl.multiple_of(partner * chunk, chunk), rows)],
            dst_ref=v_came.at[link],
            send_sem=send_sem.at[link],
            recv_sem=packed_sem.at[link],
            device_id={"head": partner},
            device_id_type=MESH,
        )

    def wait_bytes(semaphore, ref):
        pltpu.make_async_copy(ref, ref, semaphore).wait()

    def each_form(is_narrow, piece, act):
        for number in range(PACKED):

            @pl.when((is_narrow == 1) & (piece == number))
            def _(number=number):
                act(keys_of(number) * GROUP, number)

        @pl.when((is_narrow == 0) | (piece >= PACKED))
        def _():
            act(width, None)

    def weigh(first, key_first, keys):
        rows = pl.ds(first, PIECE)
        queries = jnp.concatenate(
            [q_ref[rows, g * WIDTH : (g + 1) * WIDTH] for g in range(GROUP)], axis=0
        )
        scores = lax.dot_general(
            queries, k_ref[pl.ds(key_first, keys), :], (((1,), (1,)), ((), ())),
            preferred_element_type=jnp.float32,
        )
        own = seg_col[rows, :]
        own = jnp.concatenate([own] * (keys // 128), axis=1)
        key_seg = seg_ref[0:1, pl.ds(key_first, keys)]
        key_at = key_first + lax.broadcasted_iota(jnp.int32, (PIECE, keys), 1)
        own_at = first + lax.broadcasted_iota(jnp.int32, (PIECE, keys), 0)
        allowed = (own == key_seg) & (key_at <= own_at)
        bias = jnp.where(allowed, 0.0, -jnp.inf)
        scores = scores.reshape(GROUP, PIECE, keys) + bias[None]
        row_max = jnp.max(scores, axis=-1, keepdims=True)
        return jnp.exp2((scores - row_max) * scale)

    def attend(first, key_first, blocks):
        keys = blocks * BLK
        weights = weigh(first, key_first, keys)
        total = jnp.sum(weights, axis=-1, keepdims=True)
        mixed = jnp.dot(
            weights.astype(jnp.bfloat16).reshape(GROUP * PIECE, keys),
            v_ref[pl.ds(key_first, keys), :],
            preferred_element_type=jnp.float32,
        )
        mixed = mixed.reshape(GROUP, PIECE, WIDTH) / total
        for g in range(GROUP):
            sent[pl.ds(first, PIECE), g * WIDTH : (g + 1) * WIDTH] = mixed[g].astype(jnp.bfloat16)

    def pack(first, key_first, number):
        weights = weigh(first, key_first, chunk).astype(jnp.bfloat16)
        together, keys = TOGETHER[number], keys_of(number)
        for start in range(0, GROUP, together):
            wide = jnp.concatenate([weights[start + g] for g in range(together)], axis=1)
            dense = lax.dot_general(
                wide, spread[number][...], (((1,), (1,)), ((), ())),
                preferred_element_type=jnp.float32,
            )
            sent[pl.ds(first, PIECE), start * keys : (start + together) * keys] = dense.astype(
                jnp.bfloat16
            )

    def expand(source, link):
        at = pl.multiple_of(source * width, width)
        came = v_came[link]
        came = jnp.concatenate(
            [came, jnp.zeros((WIDTH - came.shape[0], WIDTH), came.dtype)], axis=0
        )
        done = []
        for number in range(PACKED):
            together, keys = TOGETHER[number], keys_of(number)
            rows = pl.ds(number * PIECE, PIECE)
            wide = [
                jnp.dot(
                    out_ref[rows, pl.ds(pl.multiple_of(at + start * keys, 128), together * keys)],
                    spread[number][...], preferred_element_type=jnp.float32,
                )
                for start in range(0, GROUP, together)
            ]
            weights = jnp.concatenate(
                [w[:, g * WIDTH : (g + 1) * WIDTH] for w in wide for g in range(together)], axis=0
            )
            total = jnp.sum(weights, axis=-1, keepdims=True)
            mixed = jnp.dot(
                weights.astype(jnp.bfloat16), came, preferred_element_type=jnp.float32
            )
            done.append((mixed * (1.0 / total)).astype(jnp.bfloat16))
        for number in range(PACKED):
            for g in range(GROUP):
                out_ref[
                    number * PIECE : (number + 1) * PIECE,
                    pl.ds(pl.multiple_of(at + g * WIDTH, WIDTH), WIDTH),
                ] = done[number][g * PIECE : (g + 1) * PIECE]

    def one_step(step, carry):
        partner, link = pick(step, partners), pick(step, links)
        q_copy(step, partner).wait()
        block = lax.div(partner, BLK // chunk)
        blocks = light + (1 - light) * (block + 1)
        key_first = pl.multiple_of(light * block * BLK, BLK)
        is_narrow = pick(step, narrows[:-1] + [0])

        def one_piece(piece, inner):
            first = pl.multiple_of(partner * chunk + piece * PIECE, PIECE)

            def form(columns, number):
                if number is None:
                    for count in range(1, tokens // BLK + 1):

                        @pl.when(blocks == count)
                        def _(count=count):
                            attend(first, key_first if count == 1 else 0, count)
                else:
                    pack(first, key_first, number)

                @pl.when(piece == 0)
                def _():
                    admit(step)
                    if number == 0:
                        value_copy(partner, link).start()

                @pl.when(step < HEADS - 1)
                def _():
                    came = wide_sem.at[0] if number is None else packed_sem.at[link]
                    piece_copy(partner, link, piece, columns, came).start()

            each_form(is_narrow, piece, form)
            return inner

        return lax.fori_loop(0, pieces, one_piece, carry)

    lax.fori_loop(0, HEADS, one_step, 0)
    mine = pl.ds(pl.multiple_of(me * chunk, chunk), chunk)
    home = pltpu.make_async_copy(
        sent.at[mine],
        out_ref.at[:, pl.ds(pl.multiple_of(me * width, width), width)],
        in_sem.at[0],
    )
    home.start()
    home.wait()

    weight_rows = sum(keys_of(p) * GROUP * PIECE for p in range(PACKED)) // WIDTH
    packed_rows = weight_rows + keys_of(PACKED - 1)
    wide_rows = PIECE * width // WIDTH

    def unpack(at, carry):
        link = pick(at, links)
        wait_bytes(packed_sem.at[link], k_ref.at[pl.ds(0, packed_rows)])
        expand(pick(at, partners), link)
        return carry

    @pl.when(narrow_here == 1)
    def _():
        lax.fori_loop(0, HEADS - 1, unpack, 0)

    for step in range(HEADS - 1):

        @pl.when(narrows[step] == 1)
        def _(step=step):
            left = packed_rows + (pieces - PACKED) * wide_rows
            wait_bytes(send_sem.at[links[step]], k_ref.at[pl.ds(0, left)])

        @pl.when(narrows[step] == 0)
        def _(step=step):
            wait_bytes(send_sem.at[links[step]], k_ref.at[pl.ds(0, pieces * wide_rows)])

    others = pl.ds(0, (HEADS - 1) * width)

    @pl.when(narrow_here == 1)
    def _():
        wait_bytes(wide_sem.at[0], out_ref.at[pl.ds(0, (pieces - PACKED) * PIECE), others])

    @pl.when(narrow_here == 0)
    def _():
        wait_bytes(wide_sem.at[0], out_ref.at[:, others])


def on_device(queries, keys, values, segments):
    tokens, width = queries.shape
    chunk = tokens // HEADS
    return pl.pallas_call(
        kernel,
        out_shape=pltpu.VMEM((chunk, HEADS * width), queries.dtype),
        in_specs=[pl.BlockSpec(memory_space=pl.ANY)] * 4,
        out_specs=pl.BlockSpec(memory_space=pltpu.VMEM),
        scratch_shapes=[
            pltpu.VMEM(queries.shape, queries.dtype),
            pltpu.VMEM(keys.shape, keys.dtype),
            pltpu.VMEM(values.shape, values.dtype),
            pltpu.VMEM(segments.shape, segments.dtype),
            pltpu.VMEM((tokens, 128), jnp.int32),
            pltpu.VMEM(queries.shape, queries.dtype),
            pltpu.VMEM((HEADS - 1, keys_of(PACKED - 1), WIDTH), values.dtype),
            *[
                pltpu.VMEM((TOGETHER[p] * keys_of(p), TOGETHER[p] * WIDTH), queries.dtype)
                for p in range(PACKED)
            ],
            pltpu.SemaphoreType.DMA((HEADS,)),
            pltpu.SemaphoreType.DMA((3,)),
            pltpu.SemaphoreType.DMA((HEADS - 1,)),
            pltpu.SemaphoreType.DMA((1,)),
            pltpu.SemaphoreType.DMA((HEADS - 1,)),
            pltpu.SemaphoreType.REGULAR((HEADS // 2,)),
        ],
        compiler_params=pltpu.CompilerParams(
            collective_id=0, has_side_effects=True, vmem_limit_bytes=60 * 2**20
        ),
        cost_estimate=pl.CostEstimate(
            flops=4 * tokens * width * tokens, bytes_accessed=5 * 2**20,
            transcendentals=tokens * GROUP * tokens,
        ),
    )(queries, keys, values, segments)


def solution(mesh):
    placed = (P("dp", "head"), P("dp", "head"), P("dp", "head"), P("dp", None))
    return jax.shard_map(
        on_device, mesh=mesh, in_specs=placed, out_specs=P(("dp", "head"), None), check_vma=False
    )
```

```python
import jax
import jax.numpy as jnp
from jax import lax
from jax.experimental import pallas as pl
from jax.experimental.pallas import tpu as pltpu
from jax.sharding import PartitionSpec as P

HEADS = 8
WIDTH = 128
GROUP = 8
BLK = 256
PIECE = 32
MESH = pl.DeviceIdType.MESH
LOG2E = 1.4426950408889634
PACKED = 3
ORDER = (0, -3, 1, -2, 2, 3, -1)
EARLY = ((0, 3, 2, 1), (3, 2, 1, 0))
FIRST_NEAR = min(step for step, turn in enumerate(ORDER) if turn < 0)
TOGETHER = (4, 2, 4)


def keys_of(piece):
    return (piece + 1) * PIECE


def pick(step, values):
    chosen = values[-1]
    for at in range(len(values) - 2, -1, -1):
        chosen = jnp.where(step == at, values[at], chosen)
    return chosen


def kernel(
    q_hbm, k_hbm, v_hbm, seg_hbm, out_ref,
    q_ref, k_ref, v_ref, seg_ref, seg_col, sent, v_came, spread_0, spread_1, spread_2,
    q_sem, in_sem, send_sem, wide_sem, packed_sem, ready,
):
    tokens, width = q_ref.shape
    chunk = tokens // HEADS
    pieces = chunk // PIECE
    half = HEADS // 2
    spread = (spread_0, spread_1, spread_2)
    scale = WIDTH**-0.5 * LOG2E
    me = lax.axis_index("head")
    replica = lax.axis_index("dp")
    replicas = lax.axis_size("dp")
    ones = 0
    for bit in range((replicas - 1).bit_length()):
        ones = ones + lax.rem(lax.div(replica, 2**bit), 2)
    light = lax.rem(ones, 2)

    def narrow(at):
        even = 1 - lax.rem(at, BLK // chunk)
        first = 1 - lax.div(at + HEADS - 1, HEADS)
        return light * even + (1 - light) * first

    flip = lax.div(replica, replicas // 2)
    place = me + flip * (HEADS - 1 - 2 * me)
    late = lax.div(place, half)
    within = place - half * late
    low = lax.rem(within, 2)
    high = lax.div(within, 2)

    def mixed_with(i):
        return (1 - low if i % 2 else low) + 2 * (1 - high if i // 2 else high)

    def device(at):
        return at + flip * (HEADS - 1 - 2 * at)

    kind = (1 - late) * (1 + flip)
    partners, links = [], []
    for turn in ORDER:
        if turn >= 0:
            orders = (turn, EARLY[0][turn], EARLY[1][turn])
            partners.append(device(pick(kind, orders) + half * (1 - late)))
            links.append(half - 1 + pick(kind, [mixed_with(at) for at in orders]))
        else:
            partners.append(device(half * late + mixed_with(-turn)))
            links.append(-turn - 1)
    partners.append(me)
    links.append(0)
    narrows = [narrow(at) for at in partners]
    narrow_here = narrow(me)

    def q_copy(step, partner):
        rows = pl.ds(pl.multiple_of(partner * chunk, chunk), chunk)
        return pltpu.make_async_copy(q_hbm.at[rows], q_ref.at[rows], q_sem.at[step])

    def greet(at, semaphore):
        pl.semaphore_signal(
            semaphore, inc=1, device_id={"head": device(at)}, device_id_type=MESH
        )

    barrier = pltpu.get_barrier_semaphore()

    @pl.when(late == 0)
    def _():
        for at in range(half, HEADS):
            greet(at, barrier)

    @pl.when(place == half)
    def _():
        for at in range(half):
            greet(at, barrier)

    seg_copy = pltpu.make_async_copy(seg_hbm, seg_ref, in_sem.at[2])
    k_copy = pltpu.make_async_copy(k_hbm, k_ref, in_sem.at[0])
    v_copy = pltpu.make_async_copy(v_hbm, v_ref, in_sem.at[1])
    seg_copy.start()
    q_copy(0, partners[0]).start()
    k_copy.start()
    v_copy.start()
    for step in range(1, HEADS):
        q_copy(step, partners[step]).start()
    @pl.when(late == 1)
    def _():
        pl.semaphore_wait(barrier, half)
        for at in range(half):
            greet(at, ready.at[place - half])

    seg_copy.wait()
    for part in range(tokens // 128):
        row = seg_ref[0:1, part * 128 : (part + 1) * 128]
        seg_col[part * 128 : (part + 1) * 128, :] = jnp.broadcast_to(row, (128, 128)).T
    for piece in range(PACKED):
        keys = keys_of(piece)
        spread[piece][...] = jnp.zeros_like(spread[piece])
        row = lax.broadcasted_iota(jnp.int32, (keys, WIDTH), 0)
        column = lax.broadcasted_iota(jnp.int32, (keys, WIDTH), 1)
        unit = jnp.where(row == column, 1.0, 0.0).astype(jnp.bfloat16)
        for g in range(TOGETHER[piece]):
            spread[piece][g * keys : (g + 1) * keys, g * WIDTH : (g + 1) * WIDTH] = unit
    k_copy.wait()
    v_copy.wait()

    def admit(step):
        @pl.when((late == 0) & (step == 0))
        def _():
            pl.semaphore_wait(barrier, 1)

        @pl.when((late == 0) & (step == 1 - flip))
        def _():
            for at in range(half):
                pl.semaphore_wait(ready.at[at], 1)

        @pl.when((place == half - 1) & (step == 1 - flip))
        def _():
            for at in range(half, HEADS):
                greet(at, ready.at[0])

        @pl.when((late == 1) & (step == FIRST_NEAR))
        def _():
            pl.semaphore_wait(ready.at[0], 1)

    def piece_copy(partner, link, piece, columns, came):
        source = pl.ds(pl.multiple_of(partner * chunk + piece * PIECE, PIECE), PIECE)
        return pltpu.make_async_remote_copy(
            src_ref=sent.at[source, pl.ds(0, columns)],
            dst_ref=out_ref.at[
                pl.ds(pl.multiple_of(piece * PIECE, PIECE), PIECE),
                pl.ds(pl.multiple_of(me * width, width), columns),
            ],
            send_sem=send_sem.at[link],
            recv_sem=came,
            device_id={"head": partner},
            device_id_type=MESH,
        )

    def value_copy(partner, link):
        rows = keys_of(PACKED - 1)
        return pltpu.make_async_remote_copy(
            src_ref=v_ref.at[pl.ds(pl.multiple_of(partner * chunk, chunk), rows)],
            dst_ref=v_came.at[link],
            send_sem=send_sem.at[link],
            recv_sem=packed_sem.at[link],
            device_id={"head": partner},
            device_id_type=MESH,
        )

    def wait_bytes(semaphore, ref):
        pltpu.make_async_copy(ref, ref, semaphore).wait()

    def each_form(is_narrow, piece, act):
        for number in range(PACKED):

            @pl.when((is_narrow == 1) & (piece == number))
            def _(number=number):
                act(keys_of(number) * GROUP, number)

        @pl.when((is_narrow == 0) | (piece >= PACKED))
        def _():
            act(width, None)

    def weigh(first, key_first, keys):
        rows = pl.ds(first, PIECE)
        queries = jnp.concatenate(
            [q_ref[rows, g * WIDTH : (g + 1) * WIDTH] for g in range(GROUP)], axis=0
        )
        scores = lax.dot_general(
            queries, k_ref[pl.ds(key_first, keys), :], (((1,), (1,)), ((), ())),
            preferred_element_type=jnp.float32,
        )
        own = seg_col[rows, :]
        own = jnp.concatenate([own] * (keys // 128), axis=1)
        key_seg = seg_ref[0:1, pl.ds(key_first, keys)]
        key_at = key_first + lax.broadcasted_iota(jnp.int32, (PIECE, keys), 1)
        own_at = first + lax.broadcasted_iota(jnp.int32, (PIECE, keys), 0)
        allowed = (own == key_seg) & (key_at <= own_at)
        bias = jnp.where(allowed, 0.0, -jnp.inf)
        scores = scores.reshape(GROUP, PIECE, keys) + bias[None]
        row_max = jnp.max(scores, axis=-1, keepdims=True)
        return jnp.exp2((scores - row_max) * scale)

    def attend(first, key_first, blocks):
        keys = blocks * BLK
        weights = weigh(first, key_first, keys)
        total = jnp.sum(weights, axis=-1, keepdims=True)
        mixed = jnp.dot(
            weights.astype(jnp.bfloat16).reshape(GROUP * PIECE, keys),
            v_ref[pl.ds(key_first, keys), :],
            preferred_element_type=jnp.float32,
        )
        mixed = mixed.reshape(GROUP, PIECE, WIDTH) / total
        for g in range(GROUP):
            sent[pl.ds(first, PIECE), g * WIDTH : (g + 1) * WIDTH] = mixed[g].astype(jnp.bfloat16)

    def pack(first, key_first, number):
        weights = weigh(first, key_first, chunk).astype(jnp.bfloat16)
        together, keys = TOGETHER[number], keys_of(number)
        for start in range(0, GROUP, together):
            wide = jnp.concatenate([weights[start + g] for g in range(together)], axis=1)
            dense = lax.dot_general(
                wide, spread[number][...], (((1,), (1,)), ((), ())),
                preferred_element_type=jnp.float32,
            )
            sent[pl.ds(first, PIECE), start * keys : (start + together) * keys] = dense.astype(
                jnp.bfloat16
            )

    def expand(source, link):
        at = pl.multiple_of(source * width, width)
        came = v_came[link]
        came = jnp.concatenate(
            [came, jnp.zeros((WIDTH - came.shape[0], WIDTH), came.dtype)], axis=0
        )
        done = []
        for number in range(PACKED):
            together, keys = TOGETHER[number], keys_of(number)
            rows = pl.ds(number * PIECE, PIECE)
            wide = [
                jnp.dot(
                    out_ref[rows, pl.ds(pl.multiple_of(at + start * keys, 128), together * keys)],
                    spread[number][...], preferred_element_type=jnp.float32,
                )
                for start in range(0, GROUP, together)
            ]
            weights = jnp.concatenate(
                [w[:, g * WIDTH : (g + 1) * WIDTH] for w in wide for g in range(together)], axis=0
            )
            total = jnp.sum(weights, axis=-1, keepdims=True)
            mixed = jnp.dot(
                weights.astype(jnp.bfloat16), came, preferred_element_type=jnp.float32
            )
            done.append((mixed * (1.0 / total)).astype(jnp.bfloat16))
        for number in range(PACKED):
            for g in range(GROUP):
                out_ref[
                    number * PIECE : (number + 1) * PIECE,
                    pl.ds(pl.multiple_of(at + g * WIDTH, WIDTH), WIDTH),
                ] = done[number][g * PIECE : (g + 1) * PIECE]

    def one_step(step, carry):
        partner, link = pick(step, partners), pick(step, links)
        q_copy(step, partner).wait()
        block = lax.div(partner, BLK // chunk)
        blocks = light + (1 - light) * (block + 1)
        key_first = pl.multiple_of(light * block * BLK, BLK)
        is_narrow = pick(step, narrows[:-1] + [0])

        def one_piece(piece, inner):
            first = pl.multiple_of(partner * chunk + piece * PIECE, PIECE)

            def form(columns, number):
                if number is None:
                    for count in range(1, tokens // BLK + 1):

                        @pl.when(blocks == count)
                        def _(count=count):
                            attend(first, key_first if count == 1 else 0, count)
                else:
                    pack(first, key_first, number)

                @pl.when(piece == 0)
                def _():
                    admit(step)
                    if number == 0:
                        value_copy(partner, link).start()

                @pl.when(step < HEADS - 1)
                def _():
                    came = wide_sem.at[0] if number is None else packed_sem.at[link]
                    piece_copy(partner, link, piece, columns, came).start()

            each_form(is_narrow, piece, form)
            return inner

        return lax.fori_loop(0, pieces, one_piece, carry)

    lax.fori_loop(0, HEADS, one_step, 0)
    mine = pl.ds(pl.multiple_of(me * chunk, chunk), chunk)
    home = pltpu.make_async_copy(
        sent.at[mine],
        out_ref.at[:, pl.ds(pl.multiple_of(me * width, width), width)],
        in_sem.at[0],
    )
    home.start()
    home.wait()

    weight_rows = sum(keys_of(p) * GROUP * PIECE for p in range(PACKED)) // WIDTH
    packed_rows = weight_rows + keys_of(PACKED - 1)
    wide_rows = PIECE * width // WIDTH

    def unpack(at, carry):
        link = pick(at, links)
        wait_bytes(packed_sem.at[link], k_ref.at[pl.ds(0, packed_rows)])
        expand(pick(at, partners), link)
        return carry

    @pl.when(narrow_here == 1)
    def _():
        lax.fori_loop(0, HEADS - 1, unpack, 0)

    for step in range(HEADS - 1):

        @pl.when(narrows[step] == 1)
        def _(step=step):
            left = packed_rows + (pieces - PACKED) * wide_rows
            wait_bytes(send_sem.at[links[step]], k_ref.at[pl.ds(0, left)])

        @pl.when(narrows[step] == 0)
        def _(step=step):
            wait_bytes(send_sem.at[links[step]], k_ref.at[pl.ds(0, pieces * wide_rows)])

    others = pl.ds(0, (HEADS - 1) * width)

    @pl.when(narrow_here == 1)
    def _():
        wait_bytes(wide_sem.at[0], out_ref.at[pl.ds(0, (pieces - PACKED) * PIECE), others])

    @pl.when(narrow_here == 0)
    def _():
        wait_bytes(wide_sem.at[0], out_ref.at[:, others])


def on_device(queries, keys, values, segments):
    tokens, width = queries.shape
    chunk = tokens // HEADS
    return pl.pallas_call(
        kernel,
        out_shape=pltpu.VMEM((chunk, HEADS * width), queries.dtype),
        in_specs=[pl.BlockSpec(memory_space=pl.ANY)] * 4,
        out_specs=pl.BlockSpec(memory_space=pltpu.VMEM),
        scratch_shapes=[
            pltpu.VMEM(queries.shape, queries.dtype),
            pltpu.VMEM(keys.shape, keys.dtype),
            pltpu.VMEM(values.shape, values.dtype),
            pltpu.VMEM(segments.shape, segments.dtype),
            pltpu.VMEM((tokens, 128), jnp.int32),
            pltpu.VMEM(queries.shape, queries.dtype),
            pltpu.VMEM((HEADS - 1, keys_of(PACKED - 1), WIDTH), values.dtype),
            *[
                pltpu.VMEM((TOGETHER[p] * keys_of(p), TOGETHER[p] * WIDTH), queries.dtype)
                for p in range(PACKED)
            ],
            pltpu.SemaphoreType.DMA((HEADS,)),
            pltpu.SemaphoreType.DMA((3,)),
            pltpu.SemaphoreType.DMA((HEADS - 1,)),
            pltpu.SemaphoreType.DMA((1,)),
            pltpu.SemaphoreType.DMA((HEADS - 1,)),
            pltpu.SemaphoreType.REGULAR((HEADS // 2,)),
        ],
        compiler_params=pltpu.CompilerParams(
            collective_id=0, has_side_effects=True, vmem_limit_bytes=60 * 2**20
        ),
        cost_estimate=pl.CostEstimate(
            flops=4 * tokens * width * tokens, bytes_accessed=5 * 2**20,
            transcendentals=tokens * GROUP * tokens,
        ),
    )(queries, keys, values, segments)


def solution(mesh):
    placed = (P("dp", "head"), P("dp", "head"), P("dp", "head"), P("dp", None))
    return jax.shard_map(
        on_device, mesh=mesh, in_specs=placed, out_specs=P(("dp", "head"), None), check_vma=False
    )
```
